512 devices in a mesh: row: 32 (over x_lo, z, core), col: 16 (over y, x_hi).
Axes of the slice: x: 4 (x_hi: 2, x_lo: 2; x = x_hi * 2 + x_lo), y: 8, z: 8, core: 2. Of those that a mesh axis runs over, the one named last changes fastest.
Arguments:
- change: bfloat16 [16384, 53248], P('row', 'col'), may hold values from -50 to 50
- test_matrix: bfloat16 [53248, 128], P('col'), may hold values from -6 to 6
Outputs:
- scaled_left_basis: float32 [16384, 128], P(('row', 'col'))
- adapter_up_factor: float32 [16384, 128], P(('row', 'col'))
- adapter_down_factor: bfloat16 [53248, 128], P('col')
The draws below stay inside these ranges and needn't reach their ends.
All inputs are finite; a program needn't handle non-finite values.
Results may differ from the reference program's by a relative error of at most 0.012.
Values may be sent and summed in bfloat16 or wider, within the bound.
No kernel may reach another device: no remote copies, remote signals or barrier semaphores. Data moves between devices by JAX's collectives and lax.ppermute only.
A program may use at most 64 MiB of HBM per device.

```python
import math
import jax
import jax.numpy as jnp
from jax import lax

WIDTH = 16384
HIDDEN_COLUMNS = 53248
SKETCH = 128


def draw_change(key, part):
    key = jax.random.fold_in(key, 7)
    key_rows, key_cols, key_noise = jax.random.split(key, 3)
    row_scale = jnp.exp(jax.random.uniform(key_rows, (WIDTH, 1), jnp.float32, jnp.log(0.3), jnp.log(3.0)))
    col_scale = jnp.exp(jax.random.uniform(key_cols, (1, HIDDEN_COLUMNS), jnp.float32, jnp.log(0.3), jnp.log(3.0)))
    noise = jnp.clip(jax.random.normal(key_noise, (WIDTH, HIDDEN_COLUMNS), jnp.float32), -3.0, 3.0)
    return (row_scale * col_scale * noise).astype(jnp.bfloat16)


def level_of(key, shape, shards, low, largest):
    def one(axis_at, parts):
        heights = jax.random.uniform(jax.random.fold_in(jax.random.fold_in(key, 6), axis_at), (parts,), jnp.float32, low / len(shards), largest / len(shards))
        return jnp.repeat(jnp.exp(heights), shape[axis_at] // parts).reshape((-1,) + (1,) * (len(shape) - axis_at - 1))

    gain = one(*shards[0])
    for cut in shards[1:]:
        gain = gain * one(*cut)
    return gain


def centred(key, shape, scale, reach, shards=(), kind=jnp.bfloat16):
    gain = level_of(key, shape, shards, -0.22, 0.18) if shards else 1.0
    drawn = jax.random.normal(key, shape, jnp.float32) * scale * gain
    return jnp.minimum(jnp.maximum(drawn, -reach), reach).astype(kind)


def setup_inputs(seed: int = 0) -> dict:
    splits = jax.random.split(jax.random.key(seed), 3)
    return {
        "change": draw_change(jax.random.fold_in(splits[2], 71), 0),
        "test_matrix": centred(splits[1], (HIDDEN_COLUMNS, SKETCH), 1.0, 6.0, ((0, 16),)),
    }


def gram_of(tall):
    return lax.dot_general(tall.astype(jnp.float32), tall.astype(jnp.float32), (((0,), (0,)), ((), ())), precision=lax.Precision.HIGHEST, preferred_element_type=jnp.float32)

def orthonormal(tall, gram_sum):
    lower_factor = jnp.linalg.cholesky(gram_sum)
    solved = jax.scipy.linalg.solve_triangular(lower_factor, tall.T, lower=True)
    return solved.T

def reference(change, test_matrix):
    sketch = jnp.dot(change.astype(jnp.float32), test_matrix.astype(jnp.float32), preferred_element_type=jnp.float32)
    left_q32 = orthonormal(sketch, gram_of(sketch))
    scaled_left_basis = left_q32 * math.sqrt(WIDTH)
    left_q = left_q32.astype(jnp.bfloat16)
    transposed = lax.dot_general(change.astype(jnp.float32), left_q.astype(jnp.float32), (((0,), (0,)), ((), ())), preferred_element_type=jnp.float32)
    right_q32 = orthonormal(transposed, gram_of(transposed))
    right_orthonormal = right_q32.astype(jnp.bfloat16)
    adapter_down_factor = (right_orthonormal.astype(jnp.float32) * math.sqrt(HIDDEN_COLUMNS)).astype(jnp.bfloat16)
    adapter_up_factor = jnp.dot(change.astype(jnp.float32), right_orthonormal.astype(jnp.float32), preferred_element_type=jnp.float32)
    return (scaled_left_basis, adapter_up_factor, adapter_down_factor)
```

```python
import math

import jax
import jax.numpy as jnp
from jax import lax
from jax.experimental import pallas as pl
from jax.experimental.pallas import tpu as pltpu
from jax.sharding import PartitionSpec as P

WIDTH = 16384
HIDDEN_COLUMNS = 53248
SKETCH = 128
SUB = 8
BF16 = jnp.bfloat16
F32 = jnp.float32


def inverse_factor(gram):
    blocks = [gram[SUB * b : SUB * (b + 1), :] for b in range(SKETCH // SUB)]
    lane = lax.broadcasted_iota(jnp.int32, (SUB, SKETCH), 1)
    sub = lax.broadcasted_iota(jnp.int32, (SUB, SKETCH), 0)
    for j in range(SKETCH):
        b, s = divmod(j, SUB)
        row = blocks[b][s : s + 1, :]
        scaled = jnp.where(lane[:1] == j, 1.0, row) * (1.0 / row[:, j : j + 1])
        for i in range(b, SKETCH // SUB):
            if i == b and s == SUB - 1:
                continue
            below = jnp.where(lane == j, 0.0, blocks[i]) - blocks[i][:, j : j + 1] * scaled
            blocks[i] = jnp.where(sub > s, below, blocks[i]) if i == b else below
    rows = []
    for b, block in enumerate(blocks):
        on_diagonal = lane == sub + SUB * b
        pivot = jnp.sum(jnp.where(on_diagonal, block, 0.0), axis=1, keepdims=True)
        root = lax.rsqrt(pivot)
        root = root * (1.5 - 0.5 * pivot * root * root)
        rows.append(jnp.where(on_diagonal, root, jnp.where(lane < sub + SUB * b, block * root, 0.0)))
    return jnp.concatenate(rows, axis=0)


def factor_kernel(gram_ref, inverse_ref):
    inverse_ref[...] = inverse_factor(gram_ref[...])


def inverse_cholesky(gram):
    return pl.pallas_call(factor_kernel, out_shape=jax.ShapeDtypeStruct(gram.shape, F32))(gram)


def split(value):
    high = value.astype(BF16)
    return high, (value - high.astype(F32)).astype(BF16)


def times_transposed(tall, square, precision=None):
    return lax.dot_general(
        tall, square, (((1,), (1,)), ((), ())), precision=precision, preferred_element_type=F32
    )


def gram_of(tall):
    return lax.dot_general(tall, tall, (((0,), (0,)), ((), ())), preferred_element_type=F32)


def spread(value, copies):
    return jnp.broadcast_to(value[None], (copies, *value.shape))


def on_device(change, test_matrix):
    rows_dev, cols_dev = change.shape
    n_col, n_row = lax.axis_size("col"), lax.axis_size("row")
    half = n_row // 2
    share = rows_dev // n_col
    part = cols_dev // n_row
    gram_part = SKETCH // n_row
    pairs = [[2 * i, 2 * i + 1] for i in range(half)]
    same_core = [[2 * i + c for i in range(half)] for c in range(2)]

    def swap(value, axis, groups=None):
        return lax.all_to_all(value, axis, 0, 0, axis_index_groups=groups, tiled=True)

    partial = jnp.dot(change, test_matrix, preferred_element_type=F32).astype(BF16)
    pieces = swap(partial.reshape(n_col, share, SKETCH), "col")
    own_sketch = pieces.astype(F32).sum(0).astype(BF16)
    sketch = swap(spread(own_sketch, n_col), "col").reshape(rows_dev, SKETCH)

    def pack(tall, gram):
        return jnp.concatenate([tall.astype(BF16), *split(gram)], axis=-2)

    def total(packed):
        packed = packed.astype(F32).sum(0)
        tall, high, low = jnp.split(packed, (part, part + gram_part), axis=-2)
        return tall, high + low

    raw = lax.dot_general(change, sketch, (((0,), (0,)), ((), ())), preferred_element_type=F32)
    packed = pack(
        raw.reshape(2, half, part, SKETCH), gram_of(sketch).reshape(2, half, gram_part, SKETCH)
    )
    packed = pack(*total(swap(packed, "row", pairs)))
    packed = pack(*total(swap(packed, "row", same_core)))
    packed = swap(spread(packed, half), "row", same_core)
    packed = swap(spread(packed, 2), "row", pairs)
    packed = packed.reshape(n_row, part + 2 * gram_part, SKETCH)
    raw = packed[:, :part].reshape(cols_dev, SKETCH)
    left_gram = packed[:, part : part + gram_part].astype(F32) + packed[:, part + gram_part :].astype(F32)
    left_inverse = inverse_cholesky(left_gram.reshape(SKETCH, SKETCH))
    scaled_left_basis = math.sqrt(WIDTH) * times_transposed(
        own_sketch.astype(F32), left_inverse, lax.Precision.HIGHEST
    )
    high, low = split(left_inverse)
    transposed = (times_transposed(raw, high) + times_transposed(raw, low)).astype(BF16)

    core = lax.axis_index("row") % 2
    partial = jnp.dot(change, transposed, preferred_element_type=F32).reshape(n_col, share, SKETCH)
    gram_half = lax.dynamic_slice_in_dim(gram_of(transposed), core * (SKETCH // 2), SKETCH // 2, 0)
    packed = jnp.concatenate([partial, spread(gram_half, n_col)], axis=1)
    packed = swap(packed, "col").sum(0)
    right_gram = swap(spread(packed[share:], 2), "row", pairs).reshape(SKETCH, SKETCH)
    right_inverse = inverse_cholesky(right_gram)
    high, low = split(right_inverse)
    right = (times_transposed(transposed, high) + times_transposed(transposed, low)).astype(BF16)
    adapter_down_factor = (right.astype(F32) * math.sqrt(HIDDEN_COLUMNS)).astype(BF16)
    adapter_up_factor = times_transposed(packed[:share], right_inverse, lax.Precision.HIGHEST)
    return (scaled_left_basis, adapter_up_factor, adapter_down_factor)


def solution(mesh):
    in_specs = (P("row", "col"), P("col", None))
    out_specs = (P(("row", "col"), None), P(("row", "col"), None), P("col", None))
    return jax.shard_map(
        on_device, mesh=mesh, in_specs=in_specs, out_specs=out_specs, check_vma=False
    )
```
